32 devices in a mesh: dp: 4 (over x, core), expert: 8 (over z, y).
Axes of the slice: x: 2, y: 2, z: 4, core: 2. Of those that a mesh axis runs over, the one named last changes fastest.
Arguments:
- cells: bfloat16 [8192, 1024], P(('dp', 'expert')), may hold values from -6 to 6
- cell_bins: int32 [8192], P(('dp', 'expert')), may hold values from 0 to 127
- tile_counts: int32 [32, 4], P(('dp', 'expert')), may hold values from 1 to 192, 256 in all within a row
- bin_base: bfloat16 [4096, 1024], P(('dp', 'expert')), may hold values from -6 to 6
- norm_gain: float32 [1024], replicated, may hold values from 0.1 to 1.9
- expert_ids: int32 [4096, 1], P(('dp', 'expert')), may hold values from 0 to 7; in each aligned block of 128 rows (0 to 127, 128 to 255, ...) at most 24 rows name the same one
- gate_q: bfloat16 [8, 4096, 1024], P('expert', 'dp'), may hold values from -0.1875 to 0.1875
- up_q: bfloat16 [8, 4096, 1024], P('expert', 'dp'), may hold values from -0.1875 to 0.1875
- down_q: bfloat16 [8, 4096, 1024], P('expert', 'dp'), may hold values from -0.09375 to 0.09375
- gate_scales: int32 [8, 32, 8], P('expert', 'dp'), may hold values from -1 to 1
- up_scales: int32 [8, 32, 8], P('expert', 'dp'), may hold values from -1 to 1
- down_scales: int32 [8, 32, 8], P('expert', 'dp'), may hold values from -1 to 1
Outputs:
- encoded: bfloat16 [4096, 1024], P(('dp', 'expert'))
The draws below stay inside these ranges and needn't reach their ends.
Inputs may be any that keep to these rules, and one draw needn't show every extreme that they name: Each device's cells are stored grouped by tile in order of t; row s of tile_counts gives the lengths of these groups, sums to 256, and its largest entry is 192. `expert_ids`: among the 128 bins of one tile no expert is named more than 24 times, a bound that some block reaches.
All inputs are finite; a program needn't handle non-finite values.
Results may differ from the reference program's by a relative error of at most 0.014.
Values may be sent and summed in bfloat16 or wider, within the bound.
A program may use at most 64 MiB of HBM per device.

```python
import math
import jax
import jax.numpy as jnp
import numpy as np
from jax import lax

D = 1024
FF = 4096
QB = 128
TOK_DEV = 128
EXPERTS = 8
CELLS_DEV = 256
CAP = 24
CCAP = 192
HBLK = 1024
BINS = 4096
CELLS = 8192
N_DP = 4
N_EXPERT = 8


def set_ends(entries, rng, low, largest):
    index_at = [jax.random.randint(jax.random.fold_in(rng, axis), (), 0, length) for axis, length in enumerate(entries.shape)]
    widest = entries.shape.index(max(entries.shape))
    next_to = index_at[:widest] + [(index_at[widest] + 1) % entries.shape[widest]] + index_at[widest + 1:]
    return entries.at[tuple(index_at)].set(low).at[tuple(next_to)].set(largest)


def shard_levels(rng, extent, cuts, smallest, high):
    level = 1.0
    for dim, shards_of in cuts:
        draws = jax.random.uniform(jax.random.fold_in(jax.random.fold_in(rng, 6), dim), (shards_of,), jnp.float32, smallest / len(cuts), high / len(cuts))
        level = level * jnp.repeat(jnp.exp(draws), extent[dim] // shards_of).reshape((-1,) + (1,) * (len(extent) - 1 - dim))
    return level


def profile(count, total, most, slope):
    loads = [(1 << 20) // math.isqrt(rank ** slope) + 1 for rank in range(2, count + 1)]
    rest, counts = total - most - (count - 1), [1] * (count - 1)
    while rest > 0:
        candidates = [i for i in range(count - 1) if counts[i] < most]
        pool, left = sum([loads[i] for i in candidates]), rest
        for i in candidates:
            extra = min(most - counts[i], max(1, left * loads[i] // pool), rest)
            counts[i] = counts[i] + extra
            rest = rest - extra
    return np.array([most] + counts)


def ragged(own_key, amount, total, reach, lean):
    if amount == 2:
        one = jax.random.randint(own_key, (), max(1, total - reach), min(reach, total - 1) + 1)
        return jnp.stack([one, total - one])
    lengths = jnp.asarray(profile(amount, total, reach, lean), jnp.int32)
    couples = (amount - 1) // 2
    donor, taker = lengths[1:1 + 2 * couples:2], lengths[2:2 + 2 * couples:2]
    slack = jnp.minimum(donor - 1, reach - taker)
    moved = jax.random.randint(jax.random.fold_in(own_key, 1), (couples,), 0, 1 << 20) % (slack + 1)
    lengths = lengths.at[1:1 + 2 * couples:2].set(donor - moved).at[2:2 + 2 * couples:2].set(taker + moved)
    return lengths[jax.random.permutation(jax.random.fold_in(own_key, 2), amount)]


def routed_block(stream_key, own, number, rows, amount, top, bound, slope):
    ranking = jax.random.permutation(stream_key, amount)
    heavy_load, common = load_shares(amount, rows * top, bound, slope, True), load_shares(amount, rows * top, bound, slope, False)
    places = jnp.arange(amount)

    def named(sizes, offset_by):
        used = int((sizes > 0).sum())
        fixed = max(1, used // 4)
        moved = fixed + (places - fixed + offset_by * (used - fixed)) % max(1, amount - fixed)
        return jnp.zeros((amount,), jnp.int32).at[ranking[jnp.where(places < fixed, places, moved)]].set(jnp.asarray(sizes, jnp.int32))

    sizes = jnp.where(number % 4 == 0, named(heavy_load, number // 4), named(common, number - number // 4 - 1))
    mixed = jax.random.permutation(jax.random.fold_in(own, 3), amount)
    giver, taker = mixed[0:amount // 2 * 2:2], mixed[1:amount // 2 * 2:2]
    room = jnp.minimum(sizes[giver] - 1, bound - sizes[taker]) // 2
    room = jnp.where((giver == ranking[0]) | (taker == ranking[0]) | (sizes[taker] == 0), 0, jnp.maximum(room, 0))
    moved = jax.random.randint(jax.random.fold_in(own, 4), (amount // 2,), 0, 1 << 20) % (room + 1)
    sizes = sizes.at[giver].add(-moved).at[taker].add(moved)
    labels = jnp.searchsorted(jnp.cumsum(sizes), jnp.arange(rows * top), side="right").astype(jnp.int32)
    table = labels.reshape(top, rows).T
    table = table[jax.random.permutation(jax.random.fold_in(own, 1), rows)]
    offset_by = jax.random.randint(jax.random.fold_in(own, 2), (rows, 1), 0, top)
    return jnp.take_along_axis(table, (jnp.arange(top)[None, :] + offset_by) % top, axis=1)


def load_shares(number_of, total, reach, skew, full):
    portions = [(1 << 20) // math.isqrt(standing ** skew) + 1 for standing in range(1, number_of + 1)]
    largest = reach if full else min(reach, max(-(-total // number_of), total * portions[0] // sum(portions)))
    least = 1 if total - largest >= number_of - 1 else 0
    holding, surplus = [largest] + [least] * (number_of - 1), total - largest - least * (number_of - 1)
    while surplus > 0:
        free = [i for i in range(1, number_of) if holding[i] < largest] or [i for i in range(1, number_of) if holding[i] < reach]
        whole, remaining = sum([portions[i] for i in free]), surplus
        for i in free:
            extra = min(reach - holding[i], max(1, remaining * portions[i] // whole), surplus)
            holding[i] = holding[i] + extra
            surplus = surplus - extra
    return np.array(holding)


def scatter_about(stream_key, shape, deviation, limit, pieces=(), held_as=jnp.bfloat16):
    array = deviation * jax.random.normal(stream_key, shape, jnp.float32)
    if pieces:
        array = array * shard_levels(stream_key, shape, pieces, -0.22, 0.18)
    return jnp.clip(array, -limit, limit).astype(held_as)


def setup_inputs(seed: int = 0) -> dict:
    key_of = jax.random.split(jax.random.key(seed), 13)
    cells = scatter_about(key_of[0], (CELLS, D), 1.0, 6.0, ((0, 32),))
    cell_bins = set_ends(jax.random.randint(key_of[1], (CELLS,), 0, TOK_DEV), jax.random.fold_in(key_of[1], 1), 0, TOK_DEV - 1).astype(jnp.int32)
    tile_counts = jax.vmap(lambda own: ragged(own, N_DP, CELLS_DEV, CCAP, 2))(jax.random.split(key_of[2], (N_DP * N_EXPERT))).reshape((N_DP * N_EXPERT, N_DP)).astype(jnp.int32)
    bin_base = scatter_about(key_of[3], (BINS, D), 1.0, 6.0, ((0, 32),))
    norm_gain = jnp.clip(1.0 + 0.18 * jax.random.normal(key_of[4], (D,), jnp.float32), 0.1, 1.9)
    expert_ids_keys = jax.random.split(jax.random.fold_in(key_of[5], 1), BINS // TOK_DEV)
    expert_ids_turns = jax.random.permutation(jax.random.fold_in(key_of[5], 3), BINS // TOK_DEV)
    expert_ids = jax.vmap(lambda own, number: routed_block(jax.random.fold_in(key_of[5], 2), own, number, TOK_DEV, EXPERTS, 1, CAP, 2))(expert_ids_keys, expert_ids_turns).reshape((BINS, 1))
    gate_q = scatter_about(key_of[6], (EXPERTS, FF, D), D ** -0.5, 0.1875, ((0, 8), (1, 4)))
    up_q = scatter_about(key_of[7], (EXPERTS, FF, D), D ** -0.5, 0.1875, ((0, 8), (1, 4)))
    down_q = scatter_about(key_of[8], (EXPERTS, FF, D), FF ** -0.5, 0.09375, ((0, 8), (1, 4)))
    gate_scales = set_ends(jax.random.randint(key_of[9], (EXPERTS, FF // QB, D // QB), -1, 2), jax.random.fold_in(key_of[9], 1), -1, 1).astype(jnp.int32)
    up_scales = set_ends(jax.random.randint(key_of[10], (EXPERTS, FF // QB, D // QB), -1, 2), jax.random.fold_in(key_of[10], 1), -1, 1).astype(jnp.int32)
    down_scales = set_ends(jax.random.randint(key_of[11], (EXPERTS, FF // QB, D // QB), -1, 2), jax.random.fold_in(key_of[11], 1), -1, 1).astype(jnp.int32)
    return dict(cells=cells, cell_bins=cell_bins, tile_counts=tile_counts, bin_base=bin_base, norm_gain=norm_gain, expert_ids=expert_ids, gate_q=gate_q, up_q=up_q, down_q=down_q, gate_scales=gate_scales, up_scales=up_scales, down_scales=down_scales)


def dequantize(quant, scale):
    factor = jnp.exp2(scale.astype(jnp.float32))
    factor = jnp.repeat(jnp.repeat(factor, QB, axis=0), QB, axis=1).astype(jnp.bfloat16)
    return quant * factor

def reference(cells, cell_bins, tile_counts, bin_base, norm_gain, expert_ids, gate_q, up_q, down_q, gate_scales, up_scales, down_scales):
    n_devices = N_DP * N_EXPERT
    cell_pos = jnp.arange(CELLS_DEV, dtype=jnp.int32)
    run_ends = jnp.cumsum(tile_counts, axis=1).astype(jnp.int32)
    dest_tile = lax.optimization_barrier(jnp.sum((cell_pos[None, :, None] >= run_ends[:, None, :]).astype(jnp.int32), axis=2))
    source = jnp.arange(n_devices, dtype=jnp.int32)
    dest_dev = dest_tile * N_EXPERT + (source % N_EXPERT)[:, None]
    bin_index = (dest_dev * TOK_DEV + cell_bins.reshape(n_devices, CELLS_DEV)).reshape(-1).astype(jnp.int32)
    splat_sum = jax.ops.segment_sum(cells.astype(jnp.float32), bin_index, num_segments=BINS)
    residual_in = bin_base.astype(jnp.float32) + splat_sum
    mean_sq = lax.optimization_barrier(jnp.mean(residual_in * residual_in, axis=1, keepdims=True))
    normed = (residual_in * lax.rsqrt(mean_sq + 1e-06) * norm_gain[None, :]).astype(jnp.bfloat16)
    expert_col = expert_ids[:, 0].reshape(n_devices, TOK_DEV)
    one_hot = (expert_col[:, :, None] == jnp.arange(EXPERTS, dtype=jnp.int32)[None, None, :]).astype(jnp.int32)
    within = lax.optimization_barrier(jnp.sum(jnp.cumsum(one_hot, axis=1) * one_hot, axis=2)) - 1
    row_of = (source[:, None] * CAP + within).reshape(-1).astype(jnp.int32)
    expert_flat = expert_col.reshape(-1).astype(jnp.int32)
    buffer = jnp.zeros((EXPERTS, n_devices * CAP, D), jnp.bfloat16).at[expert_flat, row_of].set(normed)

    def expert_ffn(operands):
        rows_in, gq, uq, dq, gs, us, ds = operands
        w_gate = dequantize(gq, gs)
        w_up = dequantize(uq, us)
        w_down = dequantize(dq, ds)
        contract = (((1,), (1,)), ((), ()))
        gate_val = lax.dot_general(rows_in, w_gate, contract, preferred_element_type=jnp.float32)
        up_val = lax.dot_general(rows_in, w_up, contract, preferred_element_type=jnp.float32)
        hidden = (jax.nn.silu(gate_val) * up_val).astype(jnp.bfloat16)
        summed = jnp.zeros((rows_in.shape[0], D), jnp.float32)
        for block in range(N_DP):
            partial_value = jnp.dot(hidden[:, block * HBLK:(block + 1) * HBLK], w_down[block * HBLK:(block + 1) * HBLK, :], preferred_element_type=jnp.float32).astype(jnp.bfloat16)
            partial_value = lax.optimization_barrier(partial_value)
            summed = summed + partial_value.astype(jnp.float32)
        return summed.astype(jnp.bfloat16)
    results = lax.map(expert_ffn, (buffer, gate_q, up_q, down_q, gate_scales, up_scales, down_scales))
    expert_out = results[expert_flat, row_of].astype(jnp.float32)
    return (residual_in + expert_out).astype(jnp.bfloat16)
```

```python
import jax
import jax.numpy as jnp
from jax import lax
from jax.experimental import pallas as pl
from jax.experimental.pallas import tpu as pltpu
from jax.sharding import PartitionSpec as P

QB = 128


def dequantize(quant, scale):
    factor = jnp.exp2(scale.astype(jnp.float32))
    factor = jnp.repeat(jnp.repeat(factor, QB, axis=0), QB, axis=1).astype(jnp.bfloat16)
    return quant * factor


def on_device(
    cells,
    cell_bins,
    tile_counts,
    bin_base,
    norm_gain,
    expert_ids,
    gate_q,
    up_q,
    down_q,
    gate_scales,
    up_scales,
    down_scales,
):
    dp_size = lax.axis_size("dp")
    expert_count = lax.axis_size("expert") * gate_q.shape[0]
    cell_total = cells.shape[0]
    tile_bins = bin_base.shape[0]
    counts = tile_counts[0]
    run_ends = jnp.cumsum(counts)
    run_starts = run_ends - counts
    bin_iota = jnp.arange(tile_bins, dtype=jnp.int32)
    cell_cap = min(3 * cell_total // dp_size, cell_total - dp_size + 1)
    slot_iota = jnp.arange(cell_cap, dtype=jnp.int32)
    take_rows = jnp.clip(run_starts[:, None] + slot_iota[None, :], 0, cell_total - 1).reshape(-1)
    valid = (slot_iota[None, :] < counts[:, None]).reshape(-1)
    slot_rows = jnp.where(
        valid[:, None], jnp.take(cells, take_rows, axis=0), jnp.zeros((), jnp.bfloat16)
    )
    slot_bins = jnp.where(valid, jnp.take(cell_bins, take_rows), -1)
    got_rows, got_bins = (
        lax.all_to_all(slot_rows, "dp", split_axis=0, concat_axis=0, tiled=True),
        lax.all_to_all(slot_bins, "dp", split_axis=0, concat_axis=0, tiled=True),
    )
    matcher = (bin_iota[:, None] == got_bins[None, :]).astype(jnp.bfloat16)
    splat_sum = jnp.dot(matcher, got_rows, preferred_element_type=jnp.float32)
    residual_in = bin_base.astype(jnp.float32) + splat_sum
    mean_sq = jnp.mean(residual_in * residual_in, axis=1, keepdims=True)
    normed = (residual_in * lax.rsqrt(mean_sq + 1e-06) * norm_gain[None, :]).astype(jnp.bfloat16)
    capacity = max(2, 3 * tile_bins // (2 * expert_count))
    expert_col = expert_ids[:, 0]
    one_hot = (expert_col[:, None] == jnp.arange(expert_count, dtype=jnp.int32)[None, :]).astype(
        jnp.int32
    )
    within = jnp.sum(jnp.cumsum(one_hot, axis=0) * one_hot, axis=1) - 1
    slot_of = expert_col * capacity + within
    placer = (
        jnp.arange(expert_count * capacity, dtype=jnp.int32)[:, None] == slot_of[None, :]
    ).astype(jnp.bfloat16)
    outgoing = jnp.dot(placer, normed, preferred_element_type=jnp.float32).astype(jnp.bfloat16)
    arrived = lax.all_to_all(outgoing, "expert", split_axis=0, concat_axis=0, tiled=True)
    w_gate = dequantize(gate_q[0], gate_scales[0])
    w_up = dequantize(up_q[0], up_scales[0])
    w_down = dequantize(down_q[0], down_scales[0])
    contract = (((1,), (1,)), ((), ()))
    block_rows = lax.all_gather(arrived, "dp", axis=0, tiled=True)
    gate_val = lax.dot_general(block_rows, w_gate, contract, preferred_element_type=jnp.float32)
    up_val = lax.dot_general(block_rows, w_up, contract, preferred_element_type=jnp.float32)
    hidden = (jax.nn.silu(gate_val) * up_val).astype(jnp.bfloat16)
    partial_rows = jnp.dot(hidden, w_down, preferred_element_type=jnp.float32)
    summed = lax.psum_scatter(
        partial_rows.astype(jnp.bfloat16), "dp", scatter_dimension=0, tiled=True
    )
    returned = lax.all_to_all(summed, "expert", split_axis=0, concat_axis=0, tiled=True)
    expert_out = lax.dot_general(
        placer, returned, (((0,), (0,)), ((), ())), preferred_element_type=jnp.float32
    )
    return (residual_in + expert_out).astype(jnp.bfloat16)


MESH = pl.DeviceIdType.MESH
BLK = 48
NSEM = 41


def flip(value, bits):
    if bits == 1:
        return (value + 1) % 2
    high, low = value // 2, value % 2
    return 2 * ((high + bits // 2) % 2) + (low + bits % 2) % 2


def fused(
    cells, bins, counts, base, gain, ids, wg_hbm, wu_hbm, wd_hbm, sg, su, sd,
    out,
    wg, wu, wd, ids_mine, ids_sib, part, part_sib, part_x_out, part_x, resid, both,
    place, place_t, outgoing, rows_in, hidden, y32, y16, y_sib, q_out, q_in, final, back,
    send, recv, wsem,
):
    dp, ex = lax.axis_index("dp"), lax.axis_index("expert")
    x, c, z, y = dp // 2, dp % 2, ex // 2, ex % 2
    sib = (2 * x + flip(c, 1), ex)
    xpeer = (2 * flip(x, 1) + c, ex)
    y_mine = (y + c) % 2
    y_sibs = (y + 1 + c) % 2
    zk = [z] + [2 * ((z // 2 + k // 2) % 2) + (z % 2 + k % 2) % 2 for k in (1, 2, 3)]
    peer = [(dp, 2 * zk[k] + y_mine) for k in range(4)]

    loads = [
        pltpu.make_async_copy(src.at[0], dst, wsem.at[n])
        for n, (src, dst) in enumerate(((wg_hbm, wg), (wu_hbm, wu), (wd_hbm, wd)))
    ]
    for load in loads:
        load.start()

    barrier = pltpu.get_barrier_semaphore()
    for where in [sib, xpeer] + peer[1:]:
        pl.semaphore_signal(barrier, inc=1, device_id=where, device_id_type=MESH)

    @pl.when(c == 1)
    def _():
        pl.semaphore_signal(barrier, inc=1, device_id=peer[0], device_id_type=MESH)

    def rdma(src, dst, n, where):
        return pltpu.make_async_remote_copy(
            src_ref=src, dst_ref=dst, send_sem=send.at[n], recv_sem=recv.at[n],
            device_id=where, device_id_type=MESH,
        )

    f32, bf16 = jnp.float32, jnp.bfloat16
    ids_mine[...] = jnp.broadcast_to(ids[...], (8, 128))

    cell_iota = lax.broadcasted_iota(jnp.int32, (1, 256), 1)
    tile = jnp.zeros((1, 256), jnp.int32)
    run = jnp.zeros((1, 1), jnp.int32)
    for t in range(4):
        run = run + counts[:, t : t + 1]
        tile = tile + (cell_iota >= run).astype(jnp.int32)
    key = tile * 128 + bins[...]
    row_iota = lax.broadcasted_iota(jnp.int32, (128, 256), 0)

    def partial_of(t):
        hit = (row_iota + 128 * t == key).astype(f32).astype(bf16)
        return jnp.dot(hit, cells[...], preferred_element_type=f32)

    other_x, other_c = flip(x, 1), flip(c, 1)
    part[0] = partial_of(2 * other_x + other_c).astype(bf16)

    pl.semaphore_wait(barrier, 5 + c)

    c_p0 = rdma(part.at[0], part_sib.at[0], 1, sib)
    c_p0.start()
    c_ids = rdma(ids_mine, ids_sib, 0, sib)
    c_ids.start()
    part[1] = partial_of(2 * x + other_c).astype(bf16)
    c_p1 = rdma(part.at[1], part_sib.at[1], 2, sib)
    c_p1.start()
    cross = partial_of(2 * other_x + c)
    c_p0.wait_recv()
    part_x_out[...] = (cross + part_sib[0].astype(f32)).astype(bf16)
    c_px = rdma(part_x_out, part_x, 3, xpeer)
    c_px.start()
    resid[...] = base[...].astype(f32) + partial_of(2 * x + c)

    spread = (
        lax.broadcasted_iota(jnp.int32, (8, 1024), 1) // 128
        == lax.broadcasted_iota(jnp.int32, (8, 1024), 0)
    ).astype(f32)
    for n, (w, s) in enumerate(((wg, sg), (wu, su), (wd, sd))):
        loads[n].wait()
        factor = jnp.dot(
            jnp.exp2(s[0].astype(f32)).astype(bf16), spread.astype(bf16), preferred_element_type=f32
        ).astype(bf16)
        for b in range(8):
            w[b * 128 : (b + 1) * 128, :] = w[b * 128 : (b + 1) * 128, :] * jnp.broadcast_to(
                factor[b : b + 1, :], (128, 1024)
            )

    c_ids.wait_recv()
    earlier = (
        lax.broadcasted_iota(jnp.int32, (128, 128), 0)
        < lax.broadcasted_iota(jnp.int32, (128, 128), 1)
    ).astype(f32)

    def slot_of(which):
        named = (lax.broadcasted_iota(jnp.int32, (8, 128), 0) == which).astype(f32)
        before = jnp.dot(
            named.astype(bf16), earlier.astype(bf16), preferred_element_type=f32
        )
        return jnp.sum(named * before, axis=0, keepdims=True)

    mine, theirs = ids_mine[...], ids_sib[...]
    slot_mine = slot_of(mine) + (24 * c).astype(f32)
    slot_theirs = slot_of(theirs) + (24 * other_c).astype(f32)
    slot_iota = lax.broadcasted_iota(jnp.int32, (BLK, 128), 0).astype(f32)

    def placer(which, slots, expert):
        return jnp.where(
            jnp.broadcast_to(which[0:1] == expert, (BLK, 128)),
            (slot_iota == slots).astype(f32),
            0.0,
        )

    for k in range(4):
        here, there = 2 * zk[k] + y_mine, 2 * zk[k] + y_sibs
        at = slice(k * BLK, (k + 1) * BLK)
        own = placer(mine, slot_mine, here)
        place[at, 0:128] = own.astype(bf16)
        place[at, 128:256] = placer(theirs, slot_theirs, here).astype(bf16)
        pair = jnp.concatenate([own, placer(mine, slot_mine, there)], axis=0)
        place_t[k] = jnp.transpose(pair).astype(bf16)

    c_p1.wait_recv()
    resid[...] = resid[...] + part_sib[1].astype(f32)
    c_px.wait_recv()
    total = resid[...] + part_x[...].astype(f32)
    resid[...] = total
    mean_sq = jnp.mean(total * total, axis=1, keepdims=True)
    both[0:128, :] = (total * lax.rsqrt(mean_sq + 1e-06) * gain[...]).astype(bf16)
    c_n = rdma(both.at[0:128], both.at[128:256], 4, sib)
    c_n.start()
    c_n.wait_recv()
    outgoing[...] = jnp.dot(place[...], both[...], preferred_element_type=f32).astype(bf16)

    def slot(ref, k, s):
        return ref.at[k, pl.ds(s * BLK, BLK)]

    c_a = [rdma(outgoing.at[pl.ds(k * BLK, BLK)], slot(rows_in, k, 0), 5 + k, peer[k]) for k in range(4)]
    f_s1 = [rdma(slot(rows_in, k, 0), slot(rows_in, k, 1), 9 + k, sib) for k in range(4)]
    f_x2 = [rdma(slot(rows_in, k, 0), slot(rows_in, k, 2), 13 + k, xpeer) for k in range(4)]
    f_s3 = [rdma(slot(rows_in, k, 2), slot(rows_in, k, 3), 17 + k, sib) for k in range(4)]
    r_s2 = [rdma(slot(y16, k, 1), slot(y_sib, k, 1), 21 + k, sib) for k in range(4)]
    r_s0 = [rdma(slot(y16, k, 0), slot(y_sib, k, 0), 25 + k, sib) for k in range(4)]
    r_x0 = [rdma(q_out.at[k], q_in.at[k], 29 + k, xpeer) for k in range(4)]
    b_a = [rdma(final.at[k], slot(back, k, 0), 33 + k, peer[k]) for k in range(4)]
    b_s = [rdma(slot(back, k, 0), slot(back, k, 1), 37 + k, sib) for k in range(4)]

    @pl.when(c == 1)
    def _():
        c_a[0].start()

    for k in (1, 2, 3):
        c_a[k].start()

    @pl.when(c == 0)
    def _():
        rows_in[0, 0:BLK, :] = outgoing[0:BLK, :]

    def arrive(k):
        if k == 0:

            @pl.when(c == 1)
            def _():
                c_a[0].wait_recv()

        else:
            c_a[k].wait_recv()
        f_x2[k].start()
        f_s1[k].start()

    def ffn(k):
        rows = rows_in[k]
        contract = (((1,), (1,)), ((), ()))
        for j in range(0, 1024, 256):
            gate = lax.dot_general(rows, wg[j : j + 256, :], contract, preferred_element_type=f32)
            up = lax.dot_general(rows, wu[j : j + 256, :], contract, preferred_element_type=f32)
            hidden[:, j : j + 256] = (gate / (1.0 + jnp.exp(-gate)) * up).astype(bf16)
        for j in range(0, 1024, 256):
            res = jnp.dot(hidden[...], wd[:, j : j + 256], preferred_element_type=f32)
            y16[k, 0:BLK, j : j + 256] = res[BLK : 2 * BLK].astype(bf16)
            y16[k, BLK : 2 * BLK, j : j + 256] = res[3 * BLK :].astype(bf16)
            y32[k, 0:BLK, j : j + 256] = res[0:BLK]
            y32[k, BLK : 2 * BLK, j : j + 256] = res[2 * BLK : 3 * BLK]
        r_s2[k].start()
        r_s0[k].start()

    def cross_sum(k):
        r_s2[k].wait_recv()
        q_out[k] = (y32[k, BLK : 2 * BLK, :] + y_sib[k, BLK : 2 * BLK, :].astype(f32)).astype(bf16)
        r_x0[k].start()

    def finish(k):
        r_s0[k].wait_recv()
        r_x0[k].wait_recv()
        val = y32[k, 0:BLK, :] + y_sib[k, 0:BLK, :].astype(f32) + q_in[k].astype(f32)
        final[k] = val.astype(bf16)
        if k == 0:

            @pl.when(c == 1)
            def _():
                b_a[0].start()

            @pl.when(c == 0)
            def _():
                back[0, 0:BLK, :] = final[0]

        else:
            b_a[k].start()

    def returned(k):
        if k == 0:

            @pl.when(c == 1)
            def _():
                b_a[0].wait_recv()

        else:
            b_a[k].wait_recv()
        b_s[k].start()

    arrive(0)
    for k in range(4):
        if k < 3:
            arrive(k + 1)
        f_x2[k].wait_recv()
        f_s3[k].start()
        f_s1[k].wait_recv()
        f_s3[k].wait_recv()
        ffn(k)
        if k >= 1:
            cross_sum(k - 1)
        if k >= 2:
            finish(k - 2)
    cross_sum(3)
    finish(2)
    returned(0)
    returned(1)
    finish(3)
    returned(2)
    acc = resid[...]
    for k in range(4):
        if k == 3:
            returned(3)
        b_s[k].wait_recv()
        acc = acc + jnp.dot(place_t[k], back[k], preferred_element_type=f32)
    out[...] = acc.astype(bf16)

    for copy in [c_ids, c_p0, c_p1, c_px, c_n] + f_s1 + f_x2 + f_s3 + r_s2 + r_s0 + r_x0 + b_s:
        copy.wait_send()
    for copy in c_a[1:] + b_a[1:]:
        copy.wait_send()

    @pl.when(c == 1)
    def _():
        c_a[0].wait_send()
        b_a[0].wait_send()


def on_device_fused(
    cells, cell_bins, tile_counts, bin_base, norm_gain, expert_ids,
    gate_q, up_q, down_q, gate_scales, up_scales, down_scales,
):
    bf16, f32 = jnp.bfloat16, jnp.float32
    vmem, hbm = pl.BlockSpec(memory_space=pltpu.VMEM), pl.BlockSpec(memory_space=pl.ANY)
    d = 1024
    scratch = [
        pltpu.VMEM((d, d), bf16),
        pltpu.VMEM((d, d), bf16),
        pltpu.VMEM((d, d), bf16),
        pltpu.VMEM((8, 128), jnp.int32),
        pltpu.VMEM((8, 128), jnp.int32),
        pltpu.VMEM((2, 128, d), bf16),
        pltpu.VMEM((2, 128, d), bf16),
        pltpu.VMEM((128, d), bf16),
        pltpu.VMEM((128, d), bf16),
        pltpu.VMEM((128, d), f32),
        pltpu.VMEM((256, d), bf16),
        pltpu.VMEM((4 * BLK, 256), bf16),
        pltpu.VMEM((4, 128, 2 * BLK), bf16),
        pltpu.VMEM((4 * BLK, d), bf16),
        pltpu.VMEM((4, 4 * BLK, d), bf16),
        pltpu.VMEM((4 * BLK, d), bf16),
        pltpu.VMEM((4, 2 * BLK, d), f32),
        pltpu.VMEM((4, 2 * BLK, d), bf16),
        pltpu.VMEM((4, 2 * BLK, d), bf16),
        pltpu.VMEM((4, BLK, d), bf16),
        pltpu.VMEM((4, BLK, d), bf16),
        pltpu.VMEM((4, BLK, d), bf16),
        pltpu.VMEM((4, 2 * BLK, d), bf16),
        pltpu.SemaphoreType.DMA((NSEM,)),
        pltpu.SemaphoreType.DMA((NSEM,)),
        pltpu.SemaphoreType.DMA((3,)),
    ]
    return pl.pallas_call(
        fused,
        out_shape=jax.ShapeDtypeStruct(bin_base.shape, bf16),
        in_specs=[vmem] * 6 + [hbm] * 3 + [vmem] * 3,
        out_specs=vmem,
        scratch_shapes=scratch,
        compiler_params=pltpu.CompilerParams(
            collective_id=0, has_side_effects=True, vmem_limit_bytes=48 * 1024 * 1024
        ),
        cost_estimate=pl.CostEstimate(
            flops=6 * 768 * d * d, bytes_accessed=8 * d * d, transcendentals=768 * d
        ),
    )(
        cells, cell_bins.reshape(1, -1), tile_counts, bin_base, norm_gain.reshape(1, -1),
        expert_ids.reshape(1, -1), gate_q, up_q, down_q, gate_scales, up_scales, down_scales,
    )


def solution(mesh):
    small = mesh.shape["dp"] == 4 and mesh.shape["expert"] == 8
    placed = (
        P(("dp", "expert"), None),
        P(("dp", "expert")),
        P(("dp", "expert"), None),
        P(("dp", "expert"), None),
        P(),
        P(("dp", "expert"), None),
        P("expert", "dp", None),
        P("expert", "dp", None),
        P("expert", "dp", None),
        P("expert", "dp", None),
        P("expert", "dp", None),
        P("expert", "dp", None),
    )
    return jax.shard_map(
        on_device_fused if small else on_device, mesh=mesh, in_specs=placed, out_specs=P(("dp", "expert"), None), check_vma=False
    )
```

```python
import jax
import jax.numpy as jnp
from jax import lax
from jax.experimental import pallas as pl
from jax.experimental.pallas import tpu as pltpu
from jax.sharding import PartitionSpec as P

QB = 128


def dequantize(quant, scale):
    factor = jnp.exp2(scale.astype(jnp.float32))
    factor = jnp.repeat(jnp.repeat(factor, QB, axis=0), QB, axis=1).astype(jnp.bfloat16)
    return quant * factor


def on_device(
    cells,
    cell_bins,
    tile_counts,
    bin_base,
    norm_gain,
    expert_ids,
    gate_q,
    up_q,
    down_q,
    gate_scales,
    up_scales,
    down_scales,
):
    dp_size = lax.axis_size("dp")
    expert_count = lax.axis_size("expert") * gate_q.shape[0]
    cell_total = cells.shape[0]
    tile_bins = bin_base.shape[0]
    counts = tile_counts[0]
    run_ends = jnp.cumsum(counts)
    run_starts = run_ends - counts
    bin_iota = jnp.arange(tile_bins, dtype=jnp.int32)
    cell_cap = min(3 * cell_total // dp_size, cell_total - dp_size + 1)
    slot_iota = jnp.arange(cell_cap, dtype=jnp.int32)
    take_rows = jnp.clip(run_starts[:, None] + slot_iota[None, :], 0, cell_total - 1).reshape(-1)
    valid = (slot_iota[None, :] < counts[:, None]).reshape(-1)
    slot_rows = jnp.where(
        valid[:, None], jnp.take(cells, take_rows, axis=0), jnp.zeros((), jnp.bfloat16)
    )
    slot_bins = jnp.where(valid, jnp.take(cell_bins, take_rows), -1)
    got_rows, got_bins = (
        lax.all_to_all(slot_rows, "dp", split_axis=0, concat_axis=0, tiled=True),
        lax.all_to_all(slot_bins, "dp", split_axis=0, concat_axis=0, tiled=True),
    )
    matcher = (bin_iota[:, None] == got_bins[None, :]).astype(jnp.bfloat16)
    splat_sum = jnp.dot(matcher, got_rows, preferred_element_type=jnp.float32)
    residual_in = bin_base.astype(jnp.float32) + splat_sum
    mean_sq = jnp.mean(residual_in * residual_in, axis=1, keepdims=True)
    normed = (residual_in * lax.rsqrt(mean_sq + 1e-06) * norm_gain[None, :]).astype(jnp.bfloat16)
    capacity = max(2, 3 * tile_bins // (2 * expert_count))
    expert_col = expert_ids[:, 0]
    one_hot = (expert_col[:, None] == jnp.arange(expert_count, dtype=jnp.int32)[None, :]).astype(
        jnp.int32
    )
    within = jnp.sum(jnp.cumsum(one_hot, axis=0) * one_hot, axis=1) - 1
    slot_of = expert_col * capacity + within
    placer = (
        jnp.arange(expert_count * capacity, dtype=jnp.int32)[:, None] == slot_of[None, :]
    ).astype(jnp.bfloat16)
    outgoing = jnp.dot(placer, normed, preferred_element_type=jnp.float32).astype(jnp.bfloat16)
    arrived = lax.all_to_all(outgoing, "expert", split_axis=0, concat_axis=0, tiled=True)
    w_gate = dequantize(gate_q[0], gate_scales[0])
    w_up = dequantize(up_q[0], up_scales[0])
    w_down = dequantize(down_q[0], down_scales[0])
    contract = (((1,), (1,)), ((), ()))
    block_rows = lax.all_gather(arrived, "dp", axis=0, tiled=True)
    gate_val = lax.dot_general(block_rows, w_gate, contract, preferred_element_type=jnp.float32)
    up_val = lax.dot_general(block_rows, w_up, contract, preferred_element_type=jnp.float32)
    hidden = (jax.nn.silu(gate_val) * up_val).astype(jnp.bfloat16)
    partial_rows = jnp.dot(hidden, w_down, preferred_element_type=jnp.float32)
    summed = lax.psum_scatter(
        partial_rows.astype(jnp.bfloat16), "dp", scatter_dimension=0, tiled=True
    )
    returned = lax.all_to_all(summed, "expert", split_axis=0, concat_axis=0, tiled=True)
    expert_out = lax.dot_general(
        placer, returned, (((0,), (0,)), ((), ())), preferred_element_type=jnp.float32
    )
    return (residual_in + expert_out).astype(jnp.bfloat16)


MESH = pl.DeviceIdType.MESH
BLK = 48
NSEM = 41


def flip(value, bits):
    if bits == 1:
        return (value + 1) % 2
    high, low = value // 2, value % 2
    return 2 * ((high + bits // 2) % 2) + (low + bits % 2) % 2


def fused(
    cells_hbm, bins_hbm, counts_hbm, base_hbm, gain_hbm, ids_hbm, wg_hbm, wu_hbm, wd_hbm,
    sg_hbm, su_hbm, sd_hbm,
    out,
    cells, bins, counts, base, gain, ids, sg, su, sd,
    wg, wu, wd, ids_mine, ids_sib, part, part_sib, part_x_out, part_x, resid, both,
    place, place_t, outgoing, rows_in, hidden, y32, y16, y_sib, q_out, q_in, final, back,
    send, recv, wsem,
):
    dp, ex = lax.axis_index("dp"), lax.axis_index("expert")
    x, c, z, y = dp // 2, dp % 2, ex // 2, ex % 2
    sib = (2 * x + flip(c, 1), ex)
    xpeer = (2 * flip(x, 1) + c, ex)
    y_mine = (y + c) % 2
    y_sibs = (y + 1 + c) % 2
    zk = [z] + [2 * ((z // 2 + k // 2) % 2) + (z % 2 + k % 2) % 2 for k in (1, 2, 3)]
    peer = [(dp, 2 * zk[k] + y_mine) for k in range(4)]

    loads = [
        pltpu.make_async_copy(src.at[0], dst, wsem.at[n])
        for n, (src, dst) in enumerate(((wg_hbm, wg), (wu_hbm, wu), (wd_hbm, wd)))
    ]
    first = [
        pltpu.make_async_copy(src, dst, wsem.at[3 + n])
        for n, (src, dst) in enumerate(
            (
                (bins_hbm, bins), (counts_hbm, counts), (ids_hbm, ids), (cells_hbm, cells),
                (base_hbm, base), (gain_hbm, gain), (sg_hbm, sg), (su_hbm, su), (sd_hbm, sd),
            )
        )
    ]
    for load in first + loads:
        load.start()

    barrier = pltpu.get_barrier_semaphore()
    for where in [sib, xpeer] + peer[1:]:
        pl.semaphore_signal(barrier, inc=1, device_id=where, device_id_type=MESH)

    @pl.when(c == 1)
    def _():
        pl.semaphore_signal(barrier, inc=1, device_id=peer[0], device_id_type=MESH)

    def rdma(src, dst, n, where):
        return pltpu.make_async_remote_copy(
            src_ref=src, dst_ref=dst, send_sem=send.at[n], recv_sem=recv.at[n],
            device_id=where, device_id_type=MESH,
        )

    f32, bf16 = jnp.float32, jnp.bfloat16
    for load in first[:4]:
        load.wait()
    ids_mine[...] = jnp.broadcast_to(ids[...], (8, 128))

    cell_iota = lax.broadcasted_iota(jnp.int32, (1, 256), 1)
    tile = jnp.zeros((1, 256), jnp.int32)
    run = jnp.zeros((1, 1), jnp.int32)
    for t in range(4):
        run = run + counts[:, t : t + 1]
        tile = tile + (cell_iota >= run).astype(jnp.int32)
    key = tile * 128 + bins[...]
    row_iota = lax.broadcasted_iota(jnp.int32, (128, 256), 0)

    def partial_of(t):
        hit = (row_iota + 128 * t == key).astype(f32).astype(bf16)
        return jnp.dot(hit, cells[...], preferred_element_type=f32)

    other_x, other_c = flip(x, 1), flip(c, 1)
    part[0] = partial_of(2 * other_x + other_c).astype(bf16)

    pl.semaphore_wait(barrier, 5 + c)

    c_p0 = rdma(part.at[0], part_sib.at[0], 1, sib)
    c_p0.start()
    c_ids = rdma(ids_mine, ids_sib, 0, sib)
    c_ids.start()
    part[1] = partial_of(2 * x + other_c).astype(bf16)
    c_p1 = rdma(part.at[1], part_sib.at[1], 2, sib)
    c_p1.start()
    cross = partial_of(2 * other_x + c)
    c_p0.wait_recv()
    part_x_out[...] = (cross + part_sib[0].astype(f32)).astype(bf16)
    c_px = rdma(part_x_out, part_x, 3, xpeer)
    c_px.start()
    for load in first[4:]:
        load.wait()
    resid[...] = base[...].astype(f32) + partial_of(2 * x + c)

    spread = (
        lax.broadcasted_iota(jnp.int32, (8, 1024), 1) // 128
        == lax.broadcasted_iota(jnp.int32, (8, 1024), 0)
    ).astype(f32)
    for n, (w, s) in enumerate(((wg, sg), (wu, su), (wd, sd))):
        loads[n].wait()
        factor = jnp.dot(
            jnp.exp2(s[0].astype(f32)).astype(bf16), spread.astype(bf16), preferred_element_type=f32
        ).astype(bf16)
        for b in range(8):
            w[b * 128 : (b + 1) * 128, :] = w[b * 128 : (b + 1) * 128, :] * jnp.broadcast_to(
                factor[b : b + 1, :], (128, 1024)
            )

    c_ids.wait_recv()
    earlier = (
        lax.broadcasted_iota(jnp.int32, (128, 128), 0)
        < lax.broadcasted_iota(jnp.int32, (128, 128), 1)
    ).astype(f32)

    def slot_of(which):
        named = (lax.broadcasted_iota(jnp.int32, (8, 128), 0) == which).astype(f32)
        before = jnp.dot(
            named.astype(bf16), earlier.astype(bf16), preferred_element_type=f32
        )
        return jnp.sum(named * before, axis=0, keepdims=True)

    mine, theirs = ids_mine[...], ids_sib[...]
    slot_mine = slot_of(mine) + (24 * c).astype(f32)
    slot_theirs = slot_of(theirs) + (24 * other_c).astype(f32)
    slot_iota = lax.broadcasted_iota(jnp.int32, (BLK, 128), 0).astype(f32)

    def placer(which, slots, expert):
        return jnp.where(
            jnp.broadcast_to(which[0:1] == expert, (BLK, 128)),
            (slot_iota == slots).astype(f32),
            0.0,
        )

    for k in range(4):
        here, there = 2 * zk[k] + y_mine, 2 * zk[k] + y_sibs
        at = slice(k * BLK, (k + 1) * BLK)
        own = placer(mine, slot_mine, here)
        place[at, 0:128] = own.astype(bf16)
        place[at, 128:256] = placer(theirs, slot_theirs, here).astype(bf16)
        pair = jnp.concatenate([own, placer(mine, slot_mine, there)], axis=0)
        place_t[k] = jnp.transpose(pair).astype(bf16)

    c_p1.wait_recv()
    resid[...] = resid[...] + part_sib[1].astype(f32)
    c_px.wait_recv()
    total = resid[...] + part_x[...].astype(f32)
    resid[...] = total
    mean_sq = jnp.mean(total * total, axis=1, keepdims=True)
    both[0:128, :] = (total * lax.rsqrt(mean_sq + 1e-06) * gain[...]).astype(bf16)
    c_n = rdma(both.at[0:128], both.at[128:256], 4, sib)
    c_n.start()
    c_n.wait_recv()
    outgoing[...] = jnp.dot(place[...], both[...], preferred_element_type=f32).astype(bf16)

    def slot(ref, k, s):
        return ref.at[k, pl.ds(s * BLK, BLK)]

    c_a = [rdma(outgoing.at[pl.ds(k * BLK, BLK)], slot(rows_in, k, 0), 5 + k, peer[k]) for k in range(4)]
    f_s1 = [rdma(slot(rows_in, k, 0), slot(rows_in, k, 1), 9 + k, sib) for k in range(4)]
    f_x2 = [rdma(slot(rows_in, k, 0), slot(rows_in, k, 2), 13 + k, xpeer) for k in range(4)]
    f_s3 = [rdma(slot(rows_in, k, 2), slot(rows_in, k, 3), 17 + k, sib) for k in range(4)]
    r_s2 = [rdma(slot(y16, k, 1), slot(y_sib, k, 1), 21 + k, sib) for k in range(4)]
    r_s0 = [rdma(slot(y16, k, 0), slot(y_sib, k, 0), 25 + k, sib) for k in range(4)]
    r_x0 = [rdma(q_out.at[k], q_in.at[k], 29 + k, xpeer) for k in range(4)]
    b_a = [rdma(final.at[k], slot(back, k, 0), 33 + k, peer[k]) for k in range(4)]
    b_s = [rdma(slot(back, k, 0), slot(back, k, 1), 37 + k, sib) for k in range(4)]

    @pl.when(c == 1)
    def _():
        c_a[0].start()

    for k in (1, 2, 3):
        c_a[k].start()

    @pl.when(c == 0)
    def _():
        rows_in[0, 0:BLK, :] = outgoing[0:BLK, :]

    def arrive(k):
        if k == 0:

            @pl.when(c == 1)
            def _():
                c_a[0].wait_recv()

        else:
            c_a[k].wait_recv()
        f_x2[k].start()
        f_s1[k].start()

    def ffn(k):
        rows = rows_in[k]
        contract = (((1,), (1,)), ((), ()))
        for j in range(0, 1024, 256):
            gate = lax.dot_general(rows, wg[j : j + 256, :], contract, preferred_element_type=f32)
            up = lax.dot_general(rows, wu[j : j + 256, :], contract, preferred_element_type=f32)
            hidden[:, j : j + 256] = (gate / (1.0 + jnp.exp(-gate)) * up).astype(bf16)
        for j in range(0, 1024, 256):
            res = jnp.dot(hidden[...], wd[:, j : j + 256], preferred_element_type=f32)
            y16[k, 0:BLK, j : j + 256] = res[BLK : 2 * BLK].astype(bf16)
            y16[k, BLK : 2 * BLK, j : j + 256] = res[3 * BLK :].astype(bf16)
            y32[k, 0:BLK, j : j + 256] = res[0:BLK]
            y32[k, BLK : 2 * BLK, j : j + 256] = res[2 * BLK : 3 * BLK]
        r_s2[k].start()
        r_s0[k].start()

    def cross_sum(k):
        r_s2[k].wait_recv()
        q_out[k] = (y32[k, BLK : 2 * BLK, :] + y_sib[k, BLK : 2 * BLK, :].astype(f32)).astype(bf16)
        r_x0[k].start()

    def finish(k):
        r_s0[k].wait_recv()
        r_x0[k].wait_recv()
        val = y32[k, 0:BLK, :] + y_sib[k, 0:BLK, :].astype(f32) + q_in[k].astype(f32)
        final[k] = val.astype(bf16)
        if k == 0:

            @pl.when(c == 1)
            def _():
                b_a[0].start()

            @pl.when(c == 0)
            def _():
                back[0, 0:BLK, :] = final[0]

        else:
            b_a[k].start()

    def returned(k):
        if k == 0:

            @pl.when(c == 1)
            def _():
                b_a[0].wait_recv()

        else:
            b_a[k].wait_recv()
        b_s[k].start()

    arrive(0)
    for k in range(4):
        if k < 3:
            arrive(k + 1)
        f_x2[k].wait_recv()
        f_s3[k].start()
        f_s1[k].wait_recv()
        f_s3[k].wait_recv()
        ffn(k)
        if k >= 1:
            cross_sum(k - 1)
        if k >= 2:
            finish(k - 2)
    cross_sum(3)
    finish(2)
    returned(0)
    returned(1)
    finish(3)
    returned(2)
    acc = resid[...]
    for k in range(4):
        if k == 3:
            returned(3)
        b_s[k].wait_recv()
        acc = acc + jnp.dot(place_t[k], back[k], preferred_element_type=f32)
    out[...] = acc.astype(bf16)

    for copy in [c_ids, c_p0, c_p1, c_px, c_n] + f_s1 + f_x2 + f_s3 + r_s2 + r_s0 + r_x0 + b_s:
        copy.wait_send()
    for copy in c_a[1:] + b_a[1:]:
        copy.wait_send()

    @pl.when(c == 1)
    def _():
        c_a[0].wait_send()
        b_a[0].wait_send()


def on_device_fused(
    cells, cell_bins, tile_counts, bin_base, norm_gain, expert_ids,
    gate_q, up_q, down_q, gate_scales, up_scales, down_scales,
):
    bf16, f32 = jnp.bfloat16, jnp.float32
    vmem, hbm = pl.BlockSpec(memory_space=pltpu.VMEM), pl.BlockSpec(memory_space=pl.ANY)
    d = 1024
    scratch = [
        pltpu.VMEM(cells.shape, bf16),
        pltpu.VMEM((1, 256), jnp.int32),
        pltpu.VMEM((1, 4), jnp.int32),
        pltpu.VMEM((128, d), bf16),
        pltpu.VMEM((1, d), f32),
        pltpu.VMEM((1, 128), jnp.int32),
        pltpu.VMEM((1, 8, 8), jnp.int32),
        pltpu.VMEM((1, 8, 8), jnp.int32),
        pltpu.VMEM((1, 8, 8), jnp.int32),
        pltpu.VMEM((d, d), bf16),
        pltpu.VMEM((d, d), bf16),
        pltpu.VMEM((d, d), bf16),
        pltpu.VMEM((8, 128), jnp.int32),
        pltpu.VMEM((8, 128), jnp.int32),
        pltpu.VMEM((2, 128, d), bf16),
        pltpu.VMEM((2, 128, d), bf16),
        pltpu.VMEM((128, d), bf16),
        pltpu.VMEM((128, d), bf16),
        pltpu.VMEM((128, d), f32),
        pltpu.VMEM((256, d), bf16),
        pltpu.VMEM((4 * BLK, 256), bf16),
        pltpu.VMEM((4, 128, 2 * BLK), bf16),
        pltpu.VMEM((4 * BLK, d), bf16),
        pltpu.VMEM((4, 4 * BLK, d), bf16),
        pltpu.VMEM((4 * BLK, d), bf16),
        pltpu.VMEM((4, 2 * BLK, d), f32),
        pltpu.VMEM((4, 2 * BLK, d), bf16),
        pltpu.VMEM((4, 2 * BLK, d), bf16),
        pltpu.VMEM((4, BLK, d), bf16),
        pltpu.VMEM((4, BLK, d), bf16),
        pltpu.VMEM((4, BLK, d), bf16),
        pltpu.VMEM((4, 2 * BLK, d), bf16),
        pltpu.SemaphoreType.DMA((NSEM,)),
        pltpu.SemaphoreType.DMA((NSEM,)),
        pltpu.SemaphoreType.DMA((12,)),
    ]
    return pl.pallas_call(
        fused,
        out_shape=jax.ShapeDtypeStruct(bin_base.shape, bf16),
        in_specs=[hbm] * 12,
        out_specs=vmem,
        scratch_shapes=scratch,
        compiler_params=pltpu.CompilerParams(
            collective_id=0, has_side_effects=True, vmem_limit_bytes=64 * 1024 * 1024
        ),
        cost_estimate=pl.CostEstimate(
            flops=6 * 768 * d * d, bytes_accessed=8 * d * d, transcendentals=768 * d
        ),
    )(
        cells, cell_bins.reshape(1, -1), tile_counts, bin_base, norm_gain.reshape(1, -1),
        expert_ids.reshape(1, -1), gate_q, up_q, down_q, gate_scales, up_scales, down_scales,
    )


def solution(mesh):
    small = mesh.shape["dp"] == 4 and mesh.shape["expert"] == 8
    placed = (
        P(("dp", "expert"), None),
        P(("dp", "expert")),
        P(("dp", "expert"), None),
        P(("dp", "expert"), None),
        P(),
        P(("dp", "expert"), None),
        P("expert", "dp", None),
        P("expert", "dp", None),
        P("expert", "dp", None),
        P("expert", "dp", None),
        P("expert", "dp", None),
        P("expert", "dp", None),
    )
    return jax.shard_map(
        on_device_fused if small else on_device, mesh=mesh, in_specs=placed, out_specs=P(("dp", "expert"), None), check_vma=False
    )
```
